32 devices in a mesh: face: 2 (over y), tile: 16 (over z, x, core).
Axes of the slice: x: 2, y: 2, z: 4, core: 2. Of those that a mesh axis runs over, the one named last changes fastest.
Arguments:
- state_field: bfloat16 [96, 768, 128], P('face', 'tile'), may hold values from -6 to 6
- turn_codes: int32 [2, 16, 4], P('face', 'tile'), may hold values from 0 to 3
- depth_kernel: float32 [7, 7, 128], replicated, may hold values from -0.875 to 0.875
- conv_bias: float32 [128], replicated, may hold values from -3 to 3
- norm_gain: float32 [128], replicated, may hold values from 0.5 to 1.5
- norm_shift: float32 [128], replicated, may hold values from -2 to 2
- weight_in: bfloat16 [128, 512], replicated, may hold values from -0.5 to 0.5
- bias_in: float32 [512], replicated, may hold values from -3 to 3
- weight_out: bfloat16 [512, 128], replicated, may hold values from -0.25 to 0.25
- bias_out: float32 [128], replicated, may hold values from -3 to 3
- layer_scale: float32 [128], replicated, may hold values from 0.5 to 1.5
- cotangent: bfloat16 [96, 768, 128], P('face', 'tile'), may hold values from -6 to 6
Outputs:
- block_out: bfloat16 [96, 768, 128], P('face', 'tile')
- grad_field: bfloat16 [96, 768, 128], P('face', 'tile')
- grad_weight_in: float32 [128, 512], replicated
- grad_weight_out: float32 [512, 128], replicated
- grad_kernel: float32 [7, 7, 128], replicated
The draws below stay inside these ranges and needn't reach their ends.
Inputs may be any that keep to these rules, and one draw needn't show every extreme that they name: `turn_codes`: quarter turn counts; for the south and north strips only their parity acts.
All inputs are finite; a program needn't handle non-finite values.
Results may differ from the reference program's by a relative error of at most 0.0067.
Values may be sent and summed in bfloat16 or wider, within the bound.
A program may use at most 64 MiB of HBM per device.

```python
import math
import jax
import jax.numpy as jnp
from jax import lax

C = 128
HID = 512
KS = 7
S = 48
NROWS = 96
NCOLS = 768
N_FACE = 2
N_TILE = 16


def set_ends(values, rng, least, top_value):
    extent = values.shape
    index_at = [jax.random.randint(jax.random.fold_in(rng, axis), (), 0, extent[axis]) for axis in range(len(extent))]
    values = values.at[tuple(index_at)].set(least)
    longest = extent.index(max(extent))
    index_at[longest] = (index_at[longest] + 1) % extent[longest]
    return values.at[tuple(index_at)].set(top_value)


def levels(own_key, dims, split, low, high):
    loudness = 1.0
    for position, parts in split:
        draws = jax.random.uniform(jax.random.fold_in(jax.random.fold_in(own_key, 6), position), (parts,), jnp.float32, low / len(split), high / len(split))
        loudness = loudness * jnp.repeat(jnp.exp(draws), dims[position] // parts).reshape((-1,) + (1,) * (len(dims) - 1 - position))
    return loudness


def bell_draw(own_key, shape, width, bound, split=(), kind=jnp.bfloat16):
    factor_of = levels(own_key, shape, split, -0.22, 0.18) if split else 1.0
    array = jax.random.normal(own_key, shape, jnp.float32) * width * factor_of
    return jnp.minimum(jnp.maximum(array, -bound), bound).astype(kind)


def setup_inputs(seed: int = 0) -> dict:
    streams_of = jax.random.split(jax.random.key(seed), 13)
    state_field = bell_draw(streams_of[0], (NROWS, NCOLS, C), 1.0, 6.0, ((0, 2), (1, 16)))
    turn_codes = set_ends(jax.random.randint(streams_of[1], (N_FACE, N_TILE, 4), 0, 4), jax.random.fold_in(streams_of[1], 1), 0, 3).astype(jnp.int32)
    depth_kernel = bell_draw(streams_of[2], (KS, KS, C), (KS * KS) ** -0.5, 0.875, (), jnp.float32)
    conv_bias = bell_draw(streams_of[3], (C,), 0.5, 3.0, (), jnp.float32)
    norm_gain = jnp.clip(1.0 + 0.1 * jax.random.normal(streams_of[4], (C,), jnp.float32), 0.5, 1.5)
    norm_shift = bell_draw(streams_of[5], (C,), 0.3, 2.0, (), jnp.float32)
    weight_in = bell_draw(streams_of[6], (C, HID), C ** -0.5, 0.5)
    bias_in = bell_draw(streams_of[7], (HID,), 0.5, 3.0, (), jnp.float32)
    weight_out = bell_draw(streams_of[8], (HID, C), HID ** -0.5, 0.25)
    bias_out = bell_draw(streams_of[9], (C,), 0.5, 3.0, (), jnp.float32)
    layer_scale = jnp.clip(jax.random.uniform(streams_of[10], (C,), jnp.float32, 0.5, 1.5), 0.5, 1.5)
    cotangent = bell_draw(streams_of[11], (NROWS, NCOLS, C), 1.0, 6.0, ((0, 2), (1, 16)))
    return dict(state_field=state_field, turn_codes=turn_codes, depth_kernel=depth_kernel, conv_bias=conv_bias, norm_gain=norm_gain, norm_shift=norm_shift, weight_in=weight_in, bias_in=bias_in, weight_out=weight_out, bias_out=bias_out, layer_scale=layer_scale, cotangent=cotangent)


def rotate(array_in, quarters):
    return jnp.rot90(array_in, quarters, axes=(array_in.ndim - 3, array_in.ndim - 2))

def choose(options, turn_code):
    turn_code = turn_code.reshape(turn_code.shape + (1, 1, 1))
    picked = options[0]
    for option in range(1, len(options)):
        picked = jnp.where(turn_code == option, options[option], picked)
    return picked

def side_strips(tile_in, east_turn, west_turn, margin):
    tile_side = tile_in.shape[-2]
    edge_list = [tile_in[..., :, tile_side - margin:, :], tile_in[..., tile_side - margin:, :, :], tile_in[..., :, :margin, :], tile_in[..., :margin, :, :]]
    east_strip = choose([rotate(edge_list[quarter], quarter) for quarter in range(4)], east_turn)
    west_strip = choose([rotate(edge_list[(quarter + 2) % 4], quarter) for quarter in range(4)], west_turn)
    return (west_strip, east_strip)

def end_rows(widened, south_turn, north_turn, margin):
    top_rows = widened[..., :margin, :, :]
    bottom_rows = widened[..., widened.shape[-3] - margin:, :, :]
    south_strip = choose([bottom_rows, rotate(top_rows, 2)], south_turn % 2)
    north_strip = choose([top_rows, rotate(bottom_rows, 2)], north_turn % 2)
    return (north_strip, south_strip)

def pad_all(tile_stack, turn_table, margin):
    west_strip, east_strip = side_strips(tile_stack, turn_table[..., 0], turn_table[..., 1], margin)
    widened = jnp.concatenate([jnp.roll(east_strip, 1, axis=1), tile_stack, jnp.roll(west_strip, -1, axis=1)], axis=3)
    north_strip, south_strip = end_rows(widened, turn_table[..., 2], turn_table[..., 3], margin)
    return jnp.concatenate([jnp.roll(south_strip, 1, axis=0), widened, jnp.roll(north_strip, -1, axis=0)], axis=2)

def tile_step(padded, tile_in, cotangent, depth_kernel, conv_bias, norm_gain, norm_shift, weight_in, bias_in, weight_out, bias_out, layer_scale):
    tile_side = tile_in.shape[0]
    kernel_side = depth_kernel.shape[0]
    channels = tile_in.shape[2]
    padded_f = padded.astype(jnp.float32)
    convolved = jnp.zeros(tile_in.shape, jnp.float32)
    for row_off in range(kernel_side):
        for col_off in range(kernel_side):
            convolved = convolved + padded_f[row_off:row_off + tile_side, col_off:col_off + tile_side] * depth_kernel[row_off, col_off]
    convolved = convolved + conv_bias
    center = convolved - lax.optimization_barrier(jnp.mean(convolved, axis=-1, keepdims=True))
    inverse = lax.rsqrt(lax.optimization_barrier(jnp.mean(center * center, axis=-1, keepdims=True)) + 1e-06)
    normed = center * inverse
    norm_rows = (normed * norm_gain + norm_shift).astype(jnp.bfloat16).reshape(-1, channels)
    hidden = jnp.dot(norm_rows, weight_in, preferred_element_type=jnp.float32) + bias_in
    normal_cdf = 0.5 * (1.0 + lax.erf(hidden * 0.7071067811865476))
    normal_pdf = jnp.exp(-0.5 * hidden * hidden) * 0.3989422804014327
    active = (hidden * normal_cdf).astype(jnp.bfloat16)
    mixed_out = jnp.dot(active, weight_out, preferred_element_type=jnp.float32) + bias_out
    result = (tile_in.astype(jnp.float32) + layer_scale * mixed_out.reshape(tile_in.shape)).astype(jnp.bfloat16)
    grad_mixed = (cotangent.astype(jnp.float32) * layer_scale).astype(jnp.bfloat16).reshape(-1, channels)
    grad_out = jnp.dot(active.T, grad_mixed, preferred_element_type=jnp.float32)
    grad_active = jnp.dot(grad_mixed, weight_out.T, preferred_element_type=jnp.float32)
    grad_hidden = (grad_active * (normal_cdf + hidden * normal_pdf)).astype(jnp.bfloat16)
    grad_in = jnp.dot(norm_rows.T, grad_hidden, preferred_element_type=jnp.float32)
    grad_normed = jnp.dot(grad_hidden, weight_in.T, preferred_element_type=jnp.float32).reshape(tile_in.shape) * norm_gain
    grad_conv = inverse * (grad_normed - lax.optimization_barrier(jnp.mean(grad_normed, axis=-1, keepdims=True)) - normed * lax.optimization_barrier(jnp.mean(grad_normed * normed, axis=-1, keepdims=True)))
    spread_by = kernel_side - 1
    grad_spread = jnp.pad(grad_conv, ((spread_by, spread_by), (spread_by, spread_by), (0, 0)))
    pad_side = tile_side + spread_by
    pad_grad = jnp.zeros((pad_side, pad_side, channels), jnp.float32)
    kernel_rows = []
    for row_off in range(kernel_side):
        for col_off in range(kernel_side):
            pad_grad = pad_grad + grad_spread[spread_by - row_off:spread_by - row_off + pad_side, spread_by - col_off:spread_by - col_off + pad_side] * depth_kernel[row_off, col_off]
            kernel_rows.append(lax.optimization_barrier(jnp.sum(padded_f[row_off:row_off + tile_side, col_off:col_off + tile_side] * grad_conv, axis=(0, 1))))
    grad_kern = jnp.stack(kernel_rows).reshape(kernel_side, kernel_side, channels)
    return (result, pad_grad, grad_in, grad_out, grad_kern)

def reference(state_field, turn_codes, depth_kernel, conv_bias, norm_gain, norm_shift, weight_in, bias_in, weight_out, bias_out, layer_scale, cotangent):
    margin = depth_kernel.shape[0] // 2
    channels = state_field.shape[2]

    def to_tiles(whole_array):
        return whole_array.reshape(N_FACE, S, N_TILE, S, whole_array.shape[-1]).transpose(0, 2, 1, 3, 4)

    def from_tiles(tile_stack):
        return tile_stack.transpose(0, 2, 1, 3, 4).reshape(N_FACE * S, N_TILE * S, tile_stack.shape[-1])
    tile_stack = to_tiles(state_field)
    padded, pad_transpose = jax.vjp(lambda values: pad_all(values, turn_codes, margin), tile_stack.astype(jnp.float32))
    tile_count = N_FACE * N_TILE
    flat_padded = padded.reshape((tile_count,) + padded.shape[2:])
    flat_tiles = tile_stack.reshape((tile_count,) + tile_stack.shape[2:])
    cot_tiles = to_tiles(cotangent)
    flat_cot = cot_tiles.reshape((tile_count,) + cot_tiles.shape[2:])

    def visit_tile(totals, tile_items):
        outcome = tile_step(tile_items[0], tile_items[1], tile_items[2], depth_kernel, conv_bias, norm_gain, norm_shift, weight_in, bias_in, weight_out, bias_out, layer_scale)
        return ((totals[0] + outcome[2], totals[1] + outcome[3], totals[2] + outcome[4]), (outcome[0], outcome[1]))
    start_totals = (jnp.zeros((channels, weight_in.shape[1]), jnp.float32), jnp.zeros((weight_in.shape[1], channels), jnp.float32), jnp.zeros(depth_kernel.shape, jnp.float32))
    totals, (results, pad_grads) = lax.scan(visit_tile, start_totals, (flat_padded, flat_tiles, flat_cot))
    grad_tiles = pad_transpose(pad_grads.reshape(padded.shape))[0]
    block_out = from_tiles(results.reshape(tile_stack.shape))
    grad_field = from_tiles((cot_tiles.astype(jnp.float32) + grad_tiles).astype(jnp.bfloat16))
    scale_factor = 1.0 / math.sqrt(S * S * N_FACE * N_TILE)
    return (block_out, grad_field, totals[0] * scale_factor, totals[1] * scale_factor, totals[2] * scale_factor)
```

```python
import functools
import math

import jax
import jax.numpy as jnp
from jax import lax
from jax.experimental import pallas as pl
from jax.experimental.pallas import tpu as pltpu
from jax.sharding import PartitionSpec as P


def as_sent(value):
    return jax.tree.map(lambda a: a.astype(jnp.bfloat16) if a.dtype == jnp.float32 else a, value)


def extended(value, sides, width):
    for axis, dim in sides:
        size, length = (lax.axis_size(axis), value.shape[dim])
        up = [(i, (i + 1) % size) for i in range(size)]
        down = [(j, i) for i, j in up]
        last = lax.slice_in_dim(value, length - width, length, axis=dim)
        initial = lax.slice_in_dim(value, 0, width, axis=dim)
        before = lax.ppermute(last, axis, up)
        after = lax.ppermute(initial, axis, down)
        value = jnp.concatenate([before, value, after], axis=dim)
    return value


def rotate(array_in, quarters):
    return jnp.rot90(array_in, quarters, axes=(array_in.ndim - 3, array_in.ndim - 2))


def choose(options, turn_code):
    turn_code = turn_code.reshape(turn_code.shape + (1, 1, 1))
    picked = options[0]
    for option in range(1, len(options)):
        picked = jnp.where(turn_code == option, options[option], picked)
    return picked


def side_strips(tile_in, east_turn, west_turn, margin):
    tile_side = tile_in.shape[-2]
    edge_list = [
        tile_in[..., :, tile_side - margin :, :],
        tile_in[..., tile_side - margin :, :, :],
        tile_in[..., :, :margin, :],
        tile_in[..., :margin, :, :],
    ]
    east_strip = choose([rotate(edge_list[quarter], quarter) for quarter in range(4)], east_turn)
    west_strip = choose(
        [rotate(edge_list[(quarter + 2) % 4], quarter) for quarter in range(4)], west_turn
    )
    return (west_strip, east_strip)


def end_rows(widened, south_turn, north_turn, margin):
    top_rows = widened[..., :margin, :, :]
    bottom_rows = widened[..., widened.shape[-3] - margin :, :, :]
    south_strip = choose([bottom_rows, rotate(top_rows, 2)], south_turn % 2)
    north_strip = choose([top_rows, rotate(bottom_rows, 2)], north_turn % 2)
    return (north_strip, south_strip)


def tile_step(
    padded,
    tile_in,
    cotangent,
    depth_kernel,
    conv_bias,
    norm_gain,
    norm_shift,
    weight_in,
    bias_in,
    weight_out,
    bias_out,
    layer_scale,
):
    tile_side = tile_in.shape[0]
    kernel_side = depth_kernel.shape[0]
    channels = tile_in.shape[2]
    padded_f = padded.astype(jnp.float32)
    convolved = jnp.zeros(tile_in.shape, jnp.float32)
    for row_off in range(kernel_side):
        for col_off in range(kernel_side):
            convolved = (
                convolved
                + padded_f[row_off : row_off + tile_side, col_off : col_off + tile_side]
                * depth_kernel[row_off, col_off]
            )
    convolved = convolved + conv_bias
    center = convolved - jnp.mean(convolved, axis=-1, keepdims=True)
    inverse = lax.rsqrt(jnp.mean(center * center, axis=-1, keepdims=True) + 1e-06)
    normed = center * inverse
    norm_rows = (normed * norm_gain + norm_shift).astype(jnp.bfloat16).reshape(-1, channels)
    hidden = jnp.dot(norm_rows, weight_in, preferred_element_type=jnp.float32) + bias_in
    normal_cdf = 0.5 * (1.0 + lax.erf(hidden * 0.7071067811865476))
    normal_pdf = jnp.exp(-0.5 * hidden * hidden) * 0.3989422804014327
    active = (hidden * normal_cdf).astype(jnp.bfloat16)
    mixed_out = jnp.dot(active, weight_out, preferred_element_type=jnp.float32) + bias_out
    result = (tile_in.astype(jnp.float32) + layer_scale * mixed_out.reshape(tile_in.shape)).astype(
        jnp.bfloat16
    )
    grad_mixed = (
        (cotangent.astype(jnp.float32) * layer_scale).astype(jnp.bfloat16).reshape(-1, channels)
    )
    grad_out = jnp.dot(active.T, grad_mixed, preferred_element_type=jnp.float32)
    grad_active = jnp.dot(grad_mixed, weight_out.T, preferred_element_type=jnp.float32)
    grad_hidden = (grad_active * (normal_cdf + hidden * normal_pdf)).astype(jnp.bfloat16)
    grad_in = jnp.dot(norm_rows.T, grad_hidden, preferred_element_type=jnp.float32)
    grad_normed = (
        jnp.dot(grad_hidden, weight_in.T, preferred_element_type=jnp.float32).reshape(tile_in.shape)
        * norm_gain
    )
    grad_conv = inverse * (
        grad_normed
        - jnp.mean(grad_normed, axis=-1, keepdims=True)
        - normed * jnp.mean(grad_normed * normed, axis=-1, keepdims=True)
    )
    spread_by = kernel_side - 1
    grad_spread = jnp.pad(grad_conv, ((spread_by, spread_by), (spread_by, spread_by), (0, 0)))
    pad_side = tile_side + spread_by
    pad_grad = jnp.zeros((pad_side, pad_side, channels), jnp.float32)
    kernel_rows = []
    for row_off in range(kernel_side):
        for col_off in range(kernel_side):
            pad_grad = (
                pad_grad
                + grad_spread[
                    spread_by - row_off : spread_by - row_off + pad_side,
                    spread_by - col_off : spread_by - col_off + pad_side,
                ]
                * depth_kernel[row_off, col_off]
            )
            kernel_rows.append(
                jnp.sum(
                    padded_f[row_off : row_off + tile_side, col_off : col_off + tile_side]
                    * grad_conv,
                    axis=(0, 1),
                )
            )
    grad_kern = jnp.stack(kernel_rows).reshape(kernel_side, kernel_side, channels)
    return (result, pad_grad, grad_in, grad_out, grad_kern)


MESH_ID = pl.DeviceIdType.MESH
SUB = 4


def reduce_kernel(
    n_face, n_tile, rows, scale, in_ref, out_ref, kern_ref, o_in, o_out, o_kern,
    send_buf, first_buf, second_buf, all_buf, send1, recv1, send2, recv2, send3, recv3,
):
    face, tile = lax.axis_index("face"), lax.axis_index("tile")
    n1, n2 = n_face * SUB, n_tile // SUB
    me1 = face * SUB + tile % SUB
    me2 = tile // SUB

    def peer1(offset):
        other = (me1 + offset) % n1
        return other, (other // SUB, me2 * SUB + other % SUB)

    def peer2(offset):
        other = (me2 + offset) % n2
        return (face, other * SUB + tile % SUB)

    barrier = pltpu.get_barrier_semaphore()
    for k in range(1, n1):
        pl.semaphore_signal(barrier, inc=1, device_id=peer1(k)[1], device_id_type=MESH_ID)
    for k in range(1, n2):
        pl.semaphore_signal(barrier, inc=1, device_id=peer2(k), device_id_type=MESH_ID)
    blocks = in_ref.shape[1] // 128
    for q in range(blocks):
        send_buf[q * 128 : (q + 1) * 128] = in_ref[:, q * 128 : (q + 1) * 128].astype(jnp.bfloat16)
    base = blocks * 128
    depth = out_ref.shape[0]
    send_buf[base : base + depth] = out_ref[...].astype(jnp.bfloat16)
    base2 = base + depth
    taps = kern_ref.shape[0]
    send_buf[base2 : base2 + taps] = kern_ref[...].astype(jnp.bfloat16)
    if n1 * rows > base2 + taps:
        send_buf[base2 + taps :] = jnp.zeros((n1 * rows - base2 - taps, 128), jnp.bfloat16)
    pl.semaphore_wait(barrier, n1 + n2 - 2)

    def part(index):
        return pl.ds(pl.multiple_of(index * rows, 16), rows)

    copies = []
    for k in range(1, n1):
        other, where = peer1(k)
        copies.append(pltpu.make_async_remote_copy(
            src_ref=send_buf.at[part(other)], dst_ref=first_buf.at[k - 1],
            send_sem=send1.at[k - 1], recv_sem=recv1.at[k - 1],
            device_id=where, device_id_type=MESH_ID))
        copies[-1].start()
    total = send_buf[part(me1)].astype(jnp.float32)
    for k in range(1, n1):
        copies[k - 1].wait_recv()
        total = total + first_buf[k - 1].astype(jnp.float32)
    second_buf[me2] = total.astype(jnp.bfloat16)
    copies2 = []
    for k in range(1, n2):
        copies2.append(pltpu.make_async_remote_copy(
            src_ref=second_buf.at[me2], dst_ref=second_buf.at[me2],
            send_sem=send2.at[k - 1], recv_sem=recv2.at[k - 1],
            device_id=peer2(k), device_id_type=MESH_ID))
        copies2[-1].start()
    for copy in copies2:
        copy.wait_recv()
    total = second_buf[0].astype(jnp.float32)
    for k in range(1, n2):
        total = total + second_buf[k].astype(jnp.float32)
    all_buf[part(me1)] = total.astype(jnp.bfloat16)
    copies3 = []
    for k in range(1, n1):
        copies3.append(pltpu.make_async_remote_copy(
            src_ref=all_buf.at[part(me1)], dst_ref=all_buf.at[part(me1)],
            send_sem=send3.at[k - 1], recv_sem=recv3.at[k - 1],
            device_id=peer1(k)[1], device_id_type=MESH_ID))
        copies3[-1].start()
    for copy in copies3:
        copy.wait_recv()
    for copy in copies + copies2 + copies3:
        copy.wait_send()
    for q in range(blocks):
        o_in[:, q * 128 : (q + 1) * 128] = all_buf[q * 128 : (q + 1) * 128].astype(jnp.float32) * scale
    o_out[...] = all_buf[base : base + depth].astype(jnp.float32) * scale
    o_kern[...] = all_buf[base2 : base2 + taps].astype(jnp.float32) * scale


def reduce_sums(grad_in, grad_out, grad_kern, scale):
    n_face, n_tile = lax.axis_size("face"), lax.axis_size("tile")
    n1, n2 = n_face * SUB, n_tile // SUB
    taps = -(-grad_kern.shape[0] // 16) * 16
    kern = jnp.pad(grad_kern, ((0, taps - grad_kern.shape[0]), (0, 0)))
    need = grad_in.shape[1] + grad_out.shape[0] + taps
    rows = -(-need // (16 * n1)) * 16
    vmem = pl.BlockSpec(memory_space=pltpu.VMEM)
    bf16 = jnp.bfloat16
    dma = pltpu.SemaphoreType.DMA
    o_in, o_out, o_kern = pl.pallas_call(
        functools.partial(reduce_kernel, n_face, n_tile, rows, scale),
        out_shape=(
            jax.ShapeDtypeStruct(grad_in.shape, jnp.float32),
            jax.ShapeDtypeStruct(grad_out.shape, jnp.float32),
            jax.ShapeDtypeStruct(kern.shape, jnp.float32),
        ),
        in_specs=[vmem] * 3,
        out_specs=[vmem] * 3,
        scratch_shapes=[
            pltpu.VMEM((n1 * rows, 128), bf16),
            pltpu.VMEM((n1 - 1, rows, 128), bf16),
            pltpu.VMEM((n2, rows, 128), bf16),
            pltpu.VMEM((n1 * rows, 128), bf16),
            dma((n1 - 1,)), dma((n1 - 1,)), dma((n2 - 1,)), dma((n2 - 1,)), dma((n1 - 1,)), dma((n1 - 1,)),
        ],
        compiler_params=pltpu.CompilerParams(collective_id=0, has_side_effects=True, vmem_limit_bytes=32 << 20),
    )(grad_in, grad_out, kern)
    return o_in, o_out, o_kern[: grad_kern.shape[0]]


def body(
    state_field,
    turn_codes,
    depth_kernel,
    conv_bias,
    norm_gain,
    norm_shift,
    weight_in,
    bias_in,
    weight_out,
    bias_out,
    layer_scale,
    cotangent,
):
    tile_side = state_field.shape[0]
    margin = depth_kernel.shape[0] // 2
    turn_code = turn_codes[0, 0]
    west_strip, east_strip = side_strips(state_field, turn_code[0], turn_code[1], margin)
    side_rims = extended(
        as_sent(jnp.concatenate([west_strip, east_strip], axis=1)), (("tile", 1),), margin
    )
    widened = jnp.concatenate(
        [side_rims[:, :margin], state_field, side_rims[:, side_rims.shape[1] - margin :]], axis=1
    )
    north_strip, south_strip = end_rows(widened, turn_code[2], turn_code[3], margin)
    end_rims = extended(
        as_sent(jnp.concatenate([north_strip, south_strip], axis=0)), (("face", 0),), margin
    )
    padded = jnp.concatenate(
        [end_rims[:margin], widened, end_rims[end_rims.shape[0] - margin :]], axis=0
    )
    block_out, pad_grad, grad_in, grad_out, grad_kern = tile_step(
        padded,
        state_field,
        cotangent,
        depth_kernel,
        conv_bias,
        norm_gain,
        norm_shift,
        weight_in,
        bias_in,
        weight_out,
        bias_out,
        layer_scale,
    )
    pad_side = pad_grad.shape[0]
    back_rows = extended(
        jnp.concatenate([pad_grad[:margin], pad_grad[pad_side - margin :]], axis=0).astype(
            jnp.bfloat16
        ),
        (("face", 0),),
        margin,
    ).astype(jnp.float32)
    grad_north = back_rows[:margin]
    grad_south = back_rows[back_rows.shape[0] - margin :]
    north_half = turn_code[3] % 2
    south_half = turn_code[2] % 2
    top_add = jnp.where(north_half == 0, grad_north, 0.0) + jnp.where(
        south_half == 1, rotate(grad_south, 2), 0.0
    )
    bottom_add = jnp.where(north_half == 1, rotate(grad_north, 2), 0.0) + jnp.where(
        south_half == 0, grad_south, 0.0
    )
    grad_wide = pad_grad[margin : pad_side - margin]
    grad_wide = grad_wide.at[:margin].add(top_add).at[tile_side - margin :].add(bottom_add)
    back_cols = extended(
        jnp.concatenate([grad_wide[:, :margin], grad_wide[:, pad_side - margin :]], axis=1).astype(
            jnp.bfloat16
        ),
        (("tile", 1),),
        margin,
    ).astype(jnp.float32)
    grad_west = back_cols[:, :margin]
    grad_east = back_cols[:, back_cols.shape[1] - margin :]
    edge_grads = [0.0, 0.0, 0.0, 0.0]
    for quarter in range(4):
        edge_grads[quarter] = edge_grads[quarter] + jnp.where(
            turn_code[0] == quarter, rotate(grad_east, -quarter), 0.0
        )
        edge_grads[(quarter + 2) % 4] = edge_grads[(quarter + 2) % 4] + jnp.where(
            turn_code[1] == quarter, rotate(grad_west, -quarter), 0.0
        )
    grad_cells = grad_wide[:, margin : pad_side - margin]
    grad_cells = grad_cells.at[:, tile_side - margin :].add(edge_grads[0])
    grad_cells = grad_cells.at[tile_side - margin :].add(edge_grads[1])
    grad_cells = grad_cells.at[:, :margin].add(edge_grads[2])
    grad_cells = grad_cells.at[:margin].add(edge_grads[3])
    grad_field = (cotangent.astype(jnp.float32) + grad_cells).astype(jnp.bfloat16)
    scale_factor = 1.0 / math.sqrt(
        tile_side * tile_side * lax.axis_size("face") * lax.axis_size("tile")
    )
    taps = grad_kern.shape[0] * grad_kern.shape[1]
    total_in, total_out, total_kern = reduce_sums(
        grad_in, grad_out, grad_kern.reshape(taps, -1), scale_factor
    )
    return (block_out, grad_field, total_in, total_out, total_kern.reshape(grad_kern.shape))


def solution(mesh):
    placed = (
        P("face", "tile", None),
        P("face", "tile", None),
        P(),
        P(),
        P(),
        P(),
        P(),
        P(),
        P(),
        P(),
        P(),
        P("face", "tile", None),
    )
    return jax.shard_map(
        body,
        mesh=mesh,
        in_specs=placed,
        out_specs=(P("face", "tile", None), P("face", "tile", None), P(), P(), P()),
        check_vma=False,
    )
```

```python
import functools
import math

import jax
import jax.numpy as jnp
from jax import lax
from jax.experimental import pallas as pl
from jax.experimental.pallas import tpu as pltpu
from jax.sharding import PartitionSpec as P

MESH_ID = pl.DeviceIdType.MESH
SUB = 4
F32 = jnp.float32
BF16 = jnp.bfloat16


def block_kernel(
    n_face, n_tile, rows, scale, side, ks,
    codes, x_ref, cot_ref, dk_ref, cb_ref, gain_ref, shift_ref, win_ref, bin_ref, wout_ref, bout_ref, ls_ref,
    out_ref, gf_ref, o_in, o_out, o_kern,
    xpad, xs, gs, pg, kacc, acc_in, acc_out,
    col_send, col_recv, row_send, row_recv, grow_send, grow_recv, gcol_send, gcol_recv,
    send_buf, first_buf, second_buf, all_buf,
    halo_s, halo_r, send1, recv1, send2, recv2, send3, recv3,
):
    m = ks // 2
    S = side
    wide = S + 2 * m
    C = x_ref.shape[2]
    face, tile = lax.axis_index("face"), lax.axis_index("tile")
    n1, n2 = n_face * SUB, n_tile // SUB
    me1 = face * SUB + tile % SUB
    me2 = tile // SUB
    east, west = (face, (tile + 1) % n_tile), (face, (tile + n_tile - 1) % n_tile)
    below, above = ((face + 1) % n_face, tile), ((face + n_face - 1) % n_face, tile)

    def peer1(offset):
        other = (me1 + offset) % n1
        return other, (other // SUB, me2 * SUB + other % SUB)

    def peer2(offset):
        return (face, ((me2 + offset) % n2) * SUB + tile % SUB)

    barrier = pltpu.get_barrier_semaphore()
    for where in (east, west, below, above):
        pl.semaphore_signal(barrier, inc=1, device_id=where, device_id_type=MESH_ID)
    for k in range(1, n1):
        pl.semaphore_signal(barrier, inc=1, device_id=peer1(k)[1], device_id_type=MESH_ID)
    for k in range(1, n2):
        pl.semaphore_signal(barrier, inc=1, device_id=peer2(k), device_id_type=MESH_ID)

    def remote(src, dst, sems, index, where):
        copy = pltpu.make_async_remote_copy(
            src_ref=src, dst_ref=dst, send_sem=sems[0].at[index], recv_sem=sems[1].at[index],
            device_id=where, device_id_type=MESH_ID)
        copy.start()
        return copy

    halo = (halo_s, halo_r)
    q = [codes[i] for i in range(4)]

    def mirror(n, k, total):
        r = lax.broadcasted_iota(jnp.int32, (n, k), 0)
        c = lax.broadcasted_iota(jnp.int32, (n, k), 1)
        return jnp.where(r + c == total, 1.0, 0.0).astype(BF16)

    def flip(perm, value):
        return jnp.dot(perm, value.astype(BF16), preferred_element_type=F32)

    edge = jnp.zeros((wide, 8, C), F32)
    xpad[:, 0:8] = edge
    xpad[:, S + 8 : S + 16] = edge

    @pl.loop(0, S // 8)
    def _(i):
        xpad[pl.ds(m + i * 8, 8), 8 : 8 + S] = x_ref[pl.ds(i * 8, 8)].astype(F32)

    perm_s = mirror(S, S, S - 1)

    def col(j):
        return xpad[m : m + S, 8 + j, :]

    def row(j):
        return xpad[m + j, 8 : 8 + S, :]

    def turned(code, options):
        src = jnp.where(code == 1, options[1], options[0])
        src = jnp.where(code == 2, options[2], src)
        src = jnp.where(code == 3, options[3], src)
        return jnp.where((code == 1) | (code == 2), flip(perm_s, src), src)

    cols = {j: col(j) for j in list(range(m)) + list(range(S - m, S))}
    lines = {j: row(j) for j in list(range(m)) + list(range(S - m, S))}
    for j in range(m):
        hi, lo, opp = S - m + j, m - 1 - j, S - 1 - j
        col_send[0, j] = turned(q[0], [cols[hi], lines[hi], cols[lo], lines[lo]]).astype(BF16)
        col_send[1, j] = turned(q[1], [cols[j], lines[j], cols[opp], lines[opp]]).astype(BF16)
    pl.semaphore_wait(barrier, n1 + n2 + 2)
    halo_copies = [
        remote(col_send.at[0], col_recv.at[0], halo, 0, east),
        remote(col_send.at[1], col_recv.at[1], halo, 1, west),
    ]

    rim = gs.shape[2]

    @pl.loop(0, ks)
    def _(b):
        gs[b, 0 : 2 * m] = jnp.zeros((2 * m, rim, C), F32)
        gs[b, S + 2 * m :] = jnp.zeros((2 * m, rim, C), F32)

        @pl.loop(0, S // 8)
        def _(i):
            gs[b, pl.ds(2 * m + i * 8, 8), 0:8] = jnp.zeros((8, 8, C), F32)
            gs[b, pl.ds(2 * m + i * 8, 8), S : S + 8] = jnp.zeros((8, 8, C), F32)

    kacc[...] = jnp.zeros(kacc.shape, F32)
    acc_in[...] = jnp.zeros(acc_in.shape, F32)
    acc_out[...] = jnp.zeros(acc_out.shape, F32)

    def shifted(first, count):
        for b in range(ks):
            xs[b, pl.ds(first, count)] = xpad[pl.ds(first, count), 8 - m + b : 8 - m + b + S]

    halo_copies[0].wait_recv()
    halo_copies[1].wait_recv()
    for j in range(m):
        xpad[m : m + S, 8 - m + j, :] = col_recv[0, j].astype(F32)
        xpad[m : m + S, 8 + S + j, :] = col_recv[1, j].astype(F32)
    perm_w = mirror(S + 16, S + 16, S + 15)
    for i in range(m):
        south = jnp.where(q[2] % 2 == 0, xpad[S + i], flip(perm_w, xpad[2 * m - 1 - i]))
        north = jnp.where(q[3] % 2 == 0, xpad[m + i], flip(perm_w, xpad[m + S - 1 - i]))
        row_send[0, i] = south.astype(BF16)
        row_send[1, i] = north.astype(BF16)
    halo_copies += [
        remote(row_send.at[0], row_recv.at[0], halo, 2, below),
        remote(row_send.at[1], row_recv.at[1], halo, 3, above),
    ]

    @pl.loop(0, S // 6)
    def _(i):
        shifted(m + i * 6, 6)

    halo_copies[2].wait_recv()
    halo_copies[3].wait_recv()
    xpad[0:m] = row_recv[0].astype(F32)
    xpad[m + S :] = row_recv[1].astype(F32)
    shifted(0, m)
    shifted(m + S, m)

    R = 8
    M = R * S
    contract0 = (((0,), (0,)), ((), ()))
    contract1 = (((1,), (1,)), ((), ()))

    @pl.loop(0, S // R)
    def _(i):
        i0 = i * R
        parts = []
        for s in range(0, R, 4):
            acc = jnp.zeros((4, S, C), F32)
            for a in range(ks):
                for b in range(ks):
                    acc = acc + xs[b, pl.ds(i0 + s + a, 4)] * dk_ref[a * ks + b : a * ks + b + 1]
            parts.append(acc.reshape(4 * S, C))
        conv = jnp.concatenate(parts, axis=0) + cb_ref[...]
        center = conv - jnp.mean(conv, axis=-1, keepdims=True)
        inverse = lax.rsqrt(jnp.mean(center * center, axis=-1, keepdims=True) + 1e-06)
        normed = center * inverse
        gain = gain_ref[...]
        norm_rows = (normed * gain + shift_ref[...]).astype(BF16)
        hidden = jnp.dot(norm_rows, win_ref[...], preferred_element_type=F32) + bin_ref[...]
        cdf = 0.5 * (1.0 + lax.erf(hidden * 0.7071067811865476))
        pdf = jnp.exp(-0.5 * hidden * hidden) * 0.3989422804014327
        active = (hidden * cdf).astype(BF16)
        mixed = jnp.dot(active, wout_ref[...], preferred_element_type=F32) + bout_ref[...]
        tile_in = x_ref[pl.ds(i0, R)].astype(F32).reshape(M, C)
        out_ref[pl.ds(i0, R)] = (tile_in + ls_ref[...] * mixed).astype(BF16).reshape(R, S, C)
        cot = cot_ref[pl.ds(i0, R)].astype(F32).reshape(M, C)
        grad_mixed = (cot * ls_ref[...]).astype(BF16)
        acc_out[...] += lax.dot_general(grad_mixed, active, contract0, preferred_element_type=F32)
        grad_active = lax.dot_general(grad_mixed, wout_ref[...], contract1, preferred_element_type=F32)
        grad_hidden = (grad_active * (cdf + hidden * pdf)).astype(BF16)
        acc_in[...] += lax.dot_general(norm_rows, grad_hidden, contract0, preferred_element_type=F32)
        gn = lax.dot_general(grad_hidden, win_ref[...], contract1, preferred_element_type=F32) * gain
        g = inverse * (
            gn - jnp.mean(gn, axis=-1, keepdims=True)
            - normed * jnp.mean(gn * normed, axis=-1, keepdims=True)
        )
        g = g.reshape(R, S, C)
        for b in range(ks):
            gs[b, pl.ds(i0 + 2 * m, R), b : b + S] = g

    def spread(p):
        acc = jnp.zeros((m, rim, C), F32)
        for a in range(ks):
            for b in range(ks):
                acc = acc + gs[b, pl.ds(p + 2 * m - a, m)] * dk_ref[a * ks + b : a * ks + b + 1]
        pg[pl.ds(p, m)] = acc

    @pl.loop(0, 2)
    def _(e):
        spread(e * (S + m))

    gap = jnp.zeros((m, 64 - rim, C), F32)
    grow_send[0] = jnp.concatenate([pg[0:m], gap], axis=1).astype(BF16)
    grow_send[1] = jnp.concatenate([pg[S + m :], gap], axis=1).astype(BF16)
    halo_copies += [
        remote(grow_send.at[0], grow_recv.at[0], halo, 4, above),
        remote(grow_send.at[1], grow_recv.at[1], halo, 5, below),
    ]

    @pl.loop(0, S // 4)
    def _(i):
        g = gs[0, pl.ds(i * 4 + 2 * m, 4), 0:S]
        for a in range(ks):
            for b in range(ks):
                prod = xs[b, pl.ds(i * 4 + a, 4)] * g
                kacc[a * ks + b] += jnp.sum(prod.reshape(S // 2, 8, C), axis=0)

    blocks = acc_in.shape[1] // 128
    base = blocks * 128
    for k in range(blocks):
        send_buf[k * 128 : (k + 1) * 128] = acc_in[:, k * 128 : (k + 1) * 128].astype(BF16)
        send_buf[base + k * 128 : base + (k + 1) * 128] = acc_out[:, k * 128 : (k + 1) * 128].T.astype(BF16)
    taps = kacc.shape[0]
    send_buf[2 * base : 2 * base + taps] = jnp.sum(kacc[...], axis=1).astype(BF16)
    if n1 * rows > 2 * base + taps:
        send_buf[2 * base + taps :] = jnp.zeros((n1 * rows - 2 * base - taps, 128), BF16)

    def part(index):
        return pl.ds(pl.multiple_of(index * rows, 16), rows)

    copies = []
    for k in range(1, n1):
        other, where = peer1(k)
        copies.append(remote(send_buf.at[part(other)], first_buf.at[k - 1], (send1, recv1), k - 1, where))

    third = S // m // 2

    @pl.loop(0, third)
    def _(i):
        spread(m + i * m)

    total = send_buf[part(me1)].astype(F32)
    for k in range(1, n1):
        copies[k - 1].wait_recv()
        total = total + first_buf[k - 1].astype(F32)
    second_buf[me2] = total.astype(BF16)
    copies2 = []
    for k in range(1, n2):
        copies2.append(remote(second_buf.at[me2], second_buf.at[me2], (send2, recv2), k - 1, peer2(k)))

    @pl.loop(third, S // m)
    def _(i):
        spread(m + i * m)

    halo_copies[4].wait_recv()
    halo_copies[5].wait_recv()
    perm_r = mirror(rim, 64, wide - 1)
    for i in range(m):
        top_turned = flip(perm_r, grow_recv[0, m - 1 - i])
        end_turned = flip(perm_r, grow_recv[1, m - 1 - i])
        north = grow_recv[1, i].astype(F32)[:rim]
        south = grow_recv[0, i].astype(F32)[:rim]
        pg[m + i] += jnp.where(q[3] % 2 == 0, north, 0.0) + jnp.where(q[2] % 2 == 1, top_turned, 0.0)
        pg[S + i] += jnp.where(q[3] % 2 == 1, end_turned, 0.0) + jnp.where(q[2] % 2 == 0, south, 0.0)
    for j in range(m):
        gcol_send[0, j] = pg[m : m + S, j, :].astype(BF16)
        gcol_send[1, j] = pg[m : m + S, S + m + j, :].astype(BF16)
    halo_copies += [
        remote(gcol_send.at[0], gcol_recv.at[0], halo, 6, west),
        remote(gcol_send.at[1], gcol_recv.at[1], halo, 7, east),
    ]

    for copy in copies2:
        copy.wait_recv()
    total = second_buf[0].astype(F32)
    for k in range(1, n2):
        total = total + second_buf[k].astype(F32)
    all_buf[part(me1)] = total.astype(BF16)
    copies3 = []
    for k in range(1, n1):
        copies3.append(
            remote(all_buf.at[part(me1)], all_buf.at[part(me1)], (send3, recv3), k - 1, peer1(k)[1])
        )

    halo_copies[6].wait_recv()
    halo_copies[7].wait_recv()

    def back(code, value):
        plain = value.astype(F32)
        return jnp.where((code == 1) | (code == 2), flip(perm_s, value), plain)

    from_east = [back(q[0], gcol_recv[0, j]) for j in range(m)]
    from_west = [back(q[1], gcol_recv[1, j]) for j in range(m)]

    def pair(east_code, east_value, west_code, west_value):
        return jnp.where(q[0] == east_code, east_value, 0.0) + jnp.where(q[1] == west_code, west_value, 0.0)

    for j in range(m):
        o = m - 1 - j
        hi = S - m + j
        pg[m : m + S, m + hi, :] += pair(0, from_east[j], 2, from_west[o])
        pg[m : m + S, m + j, :] += pair(2, from_east[o], 0, from_west[j])
        pg[m + hi, m : m + S, :] += pair(1, from_east[j], 3, from_west[o])
        pg[m + j, m : m + S, :] += pair(3, from_east[o], 1, from_west[j])

    @pl.loop(0, S // 8)
    def _(i):
        cells = pg[pl.ds(m + i * 8, 8), m : m + S]
        gf_ref[pl.ds(i * 8, 8)] = (cot_ref[pl.ds(i * 8, 8)].astype(F32) + cells).astype(BF16)

    for copy in copies3:
        copy.wait_recv()
    for copy in halo_copies + copies + copies2 + copies3:
        copy.wait_send()
    for k in range(blocks):
        o_in[:, k * 128 : (k + 1) * 128] = all_buf[k * 128 : (k + 1) * 128].astype(F32) * scale
    o_out[...] = all_buf[base : 2 * base].astype(F32) * scale
    o_kern[...] = all_buf[2 * base : 2 * base + taps].astype(F32) * scale


def body(
    state_field, turn_codes, depth_kernel, conv_bias, norm_gain, norm_shift,
    weight_in, bias_in, weight_out, bias_out, layer_scale, cotangent,
):
    n_face, n_tile = lax.axis_size("face"), lax.axis_size("tile")
    n1, n2 = n_face * SUB, n_tile // SUB
    S, C = state_field.shape[0], state_field.shape[2]
    ks = depth_kernel.shape[0]
    m = ks // 2
    hid = weight_in.shape[1]
    taps = -(-ks * ks // 16) * 16
    rows = -(-(2 * hid + taps) // (16 * n1)) * 16
    rim = -(-(S + 2 * m) // 8) * 8
    scale = 1.0 / math.sqrt(S * S * n_face * n_tile)
    vmem = pl.BlockSpec(memory_space=pltpu.VMEM)
    dma = pltpu.SemaphoreType.DMA
    V = pltpu.VMEM
    line = lambda v: v.reshape(1, -1)
    block_out, grad_field, g_in, g_out, g_kern = pl.pallas_call(
        functools.partial(block_kernel, n_face, n_tile, rows, scale, S, ks),
        out_shape=(
            jax.ShapeDtypeStruct(state_field.shape, BF16),
            jax.ShapeDtypeStruct(state_field.shape, BF16),
            jax.ShapeDtypeStruct(weight_in.shape, F32),
            jax.ShapeDtypeStruct(weight_out.shape, F32),
            jax.ShapeDtypeStruct((taps, C), F32),
        ),
        in_specs=[pl.BlockSpec(memory_space=pltpu.SMEM)] + [vmem] * 11,
        out_specs=[vmem] * 5,
        scratch_shapes=[
            V((S + 2 * m, S + 16, C), F32),
            V((ks, S + 2 * m, S, C), F32),
            V((ks, S + 4 * m, rim, C), F32),
            V((S + 2 * m, rim, C), F32),
            V((taps, 8, C), F32),
            V((C, hid), F32),
            V((C, hid), F32),
            V((2, m, S, C), BF16), V((2, m, S, C), BF16),
            V((2, m, S + 16, C), BF16), V((2, m, S + 16, C), BF16),
            V((2, m, 64, C), BF16), V((2, m, 64, C), BF16),
            V((2, m, S, C), BF16), V((2, m, S, C), BF16),
            V((n1 * rows, C), BF16),
            V((n1 - 1, rows, C), BF16),
            V((n2, rows, C), BF16),
            V((n1 * rows, C), BF16),
            dma((8,)), dma((8,)),
            dma((n1 - 1,)), dma((n1 - 1,)), dma((n2 - 1,)), dma((n2 - 1,)), dma((n1 - 1,)), dma((n1 - 1,)),
        ],
        compiler_params=pltpu.CompilerParams(collective_id=0, has_side_effects=True, vmem_limit_bytes=56 << 20),
    )(
        turn_codes.reshape(-1), state_field, cotangent, depth_kernel.reshape(ks * ks, C),
        line(conv_bias), line(norm_gain), line(norm_shift), weight_in, line(bias_in),
        weight_out, line(bias_out), line(layer_scale),
    )
    return (block_out, grad_field, g_in, g_out, g_kern[: ks * ks].reshape(ks, ks, C))


def solution(mesh):
    placed = (
        P("face", "tile", None),
        P("face", "tile", None),
        P(),
        P(),
        P(),
        P(),
        P(),
        P(),
        P(),
        P(),
        P(),
        P("face", "tile", None),
    )
    return jax.shard_map(
        body,
        mesh=mesh,
        in_specs=placed,
        out_specs=(P("face", "tile", None), P("face", "tile", None), P(), P(), P()),
        check_vma=False,
    )
```

```python
import functools
import math

import jax
import jax.numpy as jnp
from jax import lax
from jax.experimental import pallas as pl
from jax.experimental.pallas import tpu as pltpu
from jax.sharding import PartitionSpec as P

MESH_ID = pl.DeviceIdType.MESH
SUB = 4
F32 = jnp.float32
BF16 = jnp.bfloat16


def block_kernel(
    n_face, n_tile, rows, scale, side, ks,
    codes, x_ref, cot_ref, dk_ref, cb_ref, gain_ref, shift_ref, win_ref, bin_ref, wout_ref, bout_ref, ls_ref,
    out_ref, gf_ref, o_in, o_out, o_kern,
    xpad, xs, gs, pg, hold, kacc, acc_in, acc_out,
    col_send, col_recv, row_send, row_recv, grow_send, grow_recv, gcol_send, gcol_recv,
    send_buf, first_buf, second_buf, all_buf,
    halo_s, halo_r, send1, recv1, send2, recv2, send3, recv3,
):
    m = ks // 2
    S = side
    wide = S + 2 * m
    C = x_ref.shape[2]
    face, tile = lax.axis_index("face"), lax.axis_index("tile")
    n1, n2 = n_face * SUB, n_tile // SUB
    me1 = face * SUB + tile % SUB
    me2 = tile // SUB
    east, west = (face, (tile + 1) % n_tile), (face, (tile + n_tile - 1) % n_tile)
    below, above = ((face + 1) % n_face, tile), ((face + n_face - 1) % n_face, tile)

    def peer1(offset):
        other = (me1 + offset) % n1
        return other, (other // SUB, me2 * SUB + other % SUB)

    def peer2(offset):
        return (face, ((me2 + offset) % n2) * SUB + tile % SUB)

    barrier = pltpu.get_barrier_semaphore()
    for where in (east, west, below, above):
        pl.semaphore_signal(barrier, inc=1, device_id=where, device_id_type=MESH_ID)
    for k in range(1, n1):
        pl.semaphore_signal(barrier, inc=1, device_id=peer1(k)[1], device_id_type=MESH_ID)
    for k in range(1, n2):
        pl.semaphore_signal(barrier, inc=1, device_id=peer2(k), device_id_type=MESH_ID)

    def remote(src, dst, sems, index, where):
        copy = pltpu.make_async_remote_copy(
            src_ref=src, dst_ref=dst, send_sem=sems[0].at[index], recv_sem=sems[1].at[index],
            device_id=where, device_id_type=MESH_ID)
        copy.start()
        return copy

    halo = (halo_s, halo_r)
    q = [codes[i] for i in range(4)]

    def mirror(n, k, total):
        r = lax.broadcasted_iota(jnp.int32, (n, k), 0)
        c = lax.broadcasted_iota(jnp.int32, (n, k), 1)
        return jnp.where(r + c == total, 1.0, 0.0).astype(BF16)

    def flip(perm, value):
        return jnp.dot(perm, value.astype(BF16), preferred_element_type=F32)

    edge = jnp.zeros((wide, 8, C), F32)
    xpad[:, 0:8] = edge
    xpad[:, S + 8 : S + 16] = edge

    @pl.loop(0, S // 8)
    def _(i):
        xpad[pl.ds(m + i * 8, 8), 8 : 8 + S] = x_ref[pl.ds(i * 8, 8)].astype(F32)

    perm_s = mirror(S, S, S - 1)

    def col(j):
        return xpad[m : m + S, 8 + j, :]

    def row(j):
        return xpad[m + j, 8 : 8 + S, :]

    def turned(code, options):
        src = jnp.where(code == 1, options[1], options[0])
        src = jnp.where(code == 2, options[2], src)
        src = jnp.where(code == 3, options[3], src)
        return jnp.where((code == 1) | (code == 2), flip(perm_s, src), src)

    cols = {j: col(j) for j in list(range(m)) + list(range(S - m, S))}
    lines = {j: row(j) for j in list(range(m)) + list(range(S - m, S))}
    for j in range(m):
        hi, lo, opp = S - m + j, m - 1 - j, S - 1 - j
        col_send[0, j] = turned(q[0], [cols[hi], lines[hi], cols[lo], lines[lo]]).astype(BF16)
        col_send[1, j] = turned(q[1], [cols[j], lines[j], cols[opp], lines[opp]]).astype(BF16)
    pl.semaphore_wait(barrier, n1 + n2 + 2)
    halo_copies = [
        remote(col_send.at[0], col_recv.at[0], halo, 0, east),
        remote(col_send.at[1], col_recv.at[1], halo, 1, west),
    ]

    rim = gs.shape[2]

    @pl.loop(0, ks)
    def _(b):
        gs[b, 0 : 2 * m] = jnp.zeros((2 * m, rim, C), F32)
        gs[b, S + 2 * m :] = jnp.zeros((2 * m, rim, C), F32)

        @pl.loop(0, S // 8)
        def _(i):
            gs[b, pl.ds(2 * m + i * 8, 8), 0:8] = jnp.zeros((8, 8, C), F32)
            gs[b, pl.ds(2 * m + i * 8, 8), S : S + 8] = jnp.zeros((8, 8, C), F32)

    kacc[...] = jnp.zeros(kacc.shape, F32)
    acc_in[...] = jnp.zeros(acc_in.shape, F32)
    acc_out[...] = jnp.zeros(acc_out.shape, F32)

    def shifted(first, count):
        for b in range(ks):
            xs[b, pl.ds(first, count)] = xpad[pl.ds(first, count), 8 - m + b : 8 - m + b + S]

    halo_copies[0].wait_recv()
    halo_copies[1].wait_recv()
    for j in range(m):
        xpad[m : m + S, 8 - m + j, :] = col_recv[0, j].astype(F32)
        xpad[m : m + S, 8 + S + j, :] = col_recv[1, j].astype(F32)
    perm_w = mirror(S + 16, S + 16, S + 15)
    for i in range(m):
        south = jnp.where(q[2] % 2 == 0, xpad[S + i], flip(perm_w, xpad[2 * m - 1 - i]))
        north = jnp.where(q[3] % 2 == 0, xpad[m + i], flip(perm_w, xpad[m + S - 1 - i]))
        row_send[0, i] = south.astype(BF16)
        row_send[1, i] = north.astype(BF16)
    halo_copies += [
        remote(row_send.at[0], row_recv.at[0], halo, 2, below),
        remote(row_send.at[1], row_recv.at[1], halo, 3, above),
    ]

    @pl.loop(0, S // 6)
    def _(i):
        shifted(m + i * 6, 6)

    R = 8
    M = R * S
    contract0 = (((0,), (0,)), ((), ()))
    contract1 = (((1,), (1,)), ((), ()))

    def pointwise(i):
        i0 = i * R
        parts = []
        for s in range(0, R, 4):
            acc = jnp.zeros((4, S, C), F32)
            for a in range(ks):
                for b in range(ks):
                    acc = acc + xs[b, pl.ds(i0 + s + a, 4)] * dk_ref[a, b : b + 1]
            parts.append(acc.reshape(4 * S, C))
        conv = jnp.concatenate(parts, axis=0) + cb_ref[...]
        center = conv - jnp.mean(conv, axis=-1, keepdims=True)
        inverse = lax.rsqrt(jnp.mean(center * center, axis=-1, keepdims=True) + 1e-06)
        normed = center * inverse
        gain = gain_ref[...]
        norm_rows = (normed * gain + shift_ref[...]).astype(BF16)
        hidden = jnp.dot(norm_rows, win_ref[...], preferred_element_type=F32) + bin_ref[...]
        cdf = 0.5 * (1.0 + lax.erf(hidden * 0.7071067811865476))
        pdf = jnp.exp(-0.5 * hidden * hidden) * 0.3989422804014327
        active = (hidden * cdf).astype(BF16)
        mixed = jnp.dot(active, wout_ref[...], preferred_element_type=F32) + bout_ref[...]
        tile_in = x_ref[pl.ds(i0, R)].astype(F32).reshape(M, C)
        out_ref[pl.ds(i0, R)] = (tile_in + ls_ref[...] * mixed).astype(BF16).reshape(R, S, C)
        cot = cot_ref[pl.ds(i0, R)].astype(F32).reshape(M, C)
        grad_mixed = (cot * ls_ref[...]).astype(BF16)
        acc_out[...] += lax.dot_general(grad_mixed, active, contract0, preferred_element_type=F32)
        grad_active = lax.dot_general(grad_mixed, wout_ref[...], contract1, preferred_element_type=F32)
        grad_hidden = (grad_active * (cdf + hidden * pdf)).astype(BF16)
        acc_in[...] += lax.dot_general(norm_rows, grad_hidden, contract0, preferred_element_type=F32)
        gn = lax.dot_general(grad_hidden, win_ref[...], contract1, preferred_element_type=F32) * gain
        g = inverse * (
            gn - jnp.mean(gn, axis=-1, keepdims=True)
            - normed * jnp.mean(gn * normed, axis=-1, keepdims=True)
        )
        g = g.reshape(R, S, C)
        for b in range(ks):
            gs[b, pl.ds(i0 + 2 * m, R), b : b + S] = g

    @pl.loop(1, S // R - 1)
    def _(i):
        pointwise(i)

    halo_copies[2].wait_recv()
    halo_copies[3].wait_recv()
    xpad[0:m] = row_recv[0].astype(F32)
    xpad[m + S :] = row_recv[1].astype(F32)
    shifted(0, m)
    shifted(m + S, m)

    @pl.loop(0, 2)
    def _(e):
        pointwise(e * (S // R - 1))

    def spread(p, count, first, width):
        acc = jnp.zeros((count, width, C), F32)
        for a in range(ks):
            for b in range(ks):
                acc = acc + gs[b, pl.ds(p + 2 * m - a, count), first : first + width] * dk_ref[a, b : b + 1]
        pg[pl.ds(p, count), first : first + width] = acc

    @pl.loop(0, 2)
    def _(e):
        spread(e * (S + m), m, 0, rim)

    gap = jnp.zeros((m, 64 - rim, C), F32)
    grow_send[0] = jnp.concatenate([pg[0:m], gap], axis=1).astype(BF16)
    grow_send[1] = jnp.concatenate([pg[S + m :], gap], axis=1).astype(BF16)
    halo_copies += [
        remote(grow_send.at[0], grow_recv.at[0], halo, 4, above),
        remote(grow_send.at[1], grow_recv.at[1], halo, 5, below),
    ]

    @pl.loop(0, S // 4)
    def _(i):
        g = gs[0, pl.ds(i * 4 + 2 * m, 4), 0:S]
        for a in range(ks):
            for b in range(ks):
                prod = xs[b, pl.ds(i * 4 + a, 4)] * g
                kacc[a * ks + b] += jnp.sum(prod.reshape(S // 2, 8, C), axis=0)

    blocks = acc_in.shape[1] // 128
    base = blocks * 128
    for k in range(blocks):
        send_buf[k * 128 : (k + 1) * 128] = acc_in[:, k * 128 : (k + 1) * 128].astype(BF16)
        send_buf[base + k * 128 : base + (k + 1) * 128] = acc_out[:, k * 128 : (k + 1) * 128].T.astype(BF16)
    taps = kacc.shape[0]
    send_buf[2 * base : 2 * base + taps] = jnp.sum(kacc[...], axis=1).astype(BF16)
    if n1 * rows > 2 * base + taps:
        send_buf[2 * base + taps :] = jnp.zeros((n1 * rows - 2 * base - taps, 128), BF16)

    def part(index):
        return pl.ds(pl.multiple_of(index * rows, 16), rows)

    copies = []
    for k in range(1, n1):
        other, where = peer1(k)
        copies.append(remote(send_buf.at[part(other)], first_buf.at[k - 1], (send1, recv1), k - 1, where))

    @pl.loop(0, S // 12)
    def _(i):
        spread(m + i * 12, 12, 0, 8)
        spread(m + i * 12, 12, rim - 8, 8)

    halo_copies[4].wait_recv()
    halo_copies[5].wait_recv()
    perm_r = mirror(rim, 64, wide - 1)
    for i in range(m):
        top_turned = flip(perm_r, grow_recv[0, m - 1 - i])
        end_turned = flip(perm_r, grow_recv[1, m - 1 - i])
        north = grow_recv[1, i].astype(F32)[:rim]
        south = grow_recv[0, i].astype(F32)[:rim]
        hold[i] = jnp.where(q[3] % 2 == 0, north, 0.0) + jnp.where(q[2] % 2 == 1, top_turned, 0.0)
        hold[m + i] = jnp.where(q[3] % 2 == 1, end_turned, 0.0) + jnp.where(q[2] % 2 == 0, south, 0.0)

    def add_rows(first, width):
        for start, at in ((m, 0), (S, m)):
            pg[start : start + m, first : first + width] += hold[at : at + m, first : first + width]

    add_rows(0, 8)
    add_rows(rim - 8, 8)
    for j in range(m):
        gcol_send[0, j] = pg[m : m + S, j, :].astype(BF16)
        gcol_send[1, j] = pg[m : m + S, S + m + j, :].astype(BF16)
    halo_copies += [
        remote(gcol_send.at[0], gcol_recv.at[0], halo, 6, west),
        remote(gcol_send.at[1], gcol_recv.at[1], halo, 7, east),
    ]

    total = send_buf[part(me1)].astype(F32)
    for k in range(1, n1):
        copies[k - 1].wait_recv()
        total = total + first_buf[k - 1].astype(F32)
    second_buf[me2] = total.astype(BF16)
    copies2 = []
    for k in range(1, n2):
        copies2.append(remote(second_buf.at[me2], second_buf.at[me2], (send2, recv2), k - 1, peer2(k)))

    middle = S // 8

    @pl.loop(0, middle)
    def _(i):
        spread(m + i * 4, 4, 8, rim - 16)

    for copy in copies2:
        copy.wait_recv()
    total = second_buf[0].astype(F32)
    for k in range(1, n2):
        total = total + second_buf[k].astype(F32)
    all_buf[part(me1)] = total.astype(BF16)
    copies3 = []
    for k in range(1, n1):
        copies3.append(
            remote(all_buf.at[part(me1)], all_buf.at[part(me1)], (send3, recv3), k - 1, peer1(k)[1])
        )

    @pl.loop(middle, S // 4)
    def _(i):
        spread(m + i * 4, 4, 8, rim - 16)

    add_rows(8, rim - 16)
    halo_copies[6].wait_recv()
    halo_copies[7].wait_recv()

    def back(code, value):
        plain = value.astype(F32)
        return jnp.where((code == 1) | (code == 2), flip(perm_s, value), plain)

    from_east = [back(q[0], gcol_recv[0, j]) for j in range(m)]
    from_west = [back(q[1], gcol_recv[1, j]) for j in range(m)]

    def pair(east_code, east_value, west_code, west_value):
        return jnp.where(q[0] == east_code, east_value, 0.0) + jnp.where(q[1] == west_code, west_value, 0.0)

    for j in range(m):
        o = m - 1 - j
        hi = S - m + j
        pg[m : m + S, m + hi, :] += pair(0, from_east[j], 2, from_west[o])
        pg[m : m + S, m + j, :] += pair(2, from_east[o], 0, from_west[j])
        pg[m + hi, m : m + S, :] += pair(1, from_east[j], 3, from_west[o])
        pg[m + j, m : m + S, :] += pair(3, from_east[o], 1, from_west[j])

    @pl.loop(0, S // 8)
    def _(i):
        cells = pg[pl.ds(m + i * 8, 8), m : m + S]
        gf_ref[pl.ds(i * 8, 8)] = (cot_ref[pl.ds(i * 8, 8)].astype(F32) + cells).astype(BF16)

    for copy in copies3:
        copy.wait_recv()
    for copy in halo_copies + copies + copies2 + copies3:
        copy.wait_send()
    for k in range(blocks):
        o_in[:, k * 128 : (k + 1) * 128] = all_buf[k * 128 : (k + 1) * 128].astype(F32) * scale
    o_out[...] = all_buf[base : 2 * base].astype(F32) * scale
    kern = all_buf[2 * base : 2 * base + taps].astype(F32) * scale
    for a in range(ks):
        o_kern[a] = kern[a * ks : (a + 1) * ks]


def body(
    state_field, turn_codes, depth_kernel, conv_bias, norm_gain, norm_shift,
    weight_in, bias_in, weight_out, bias_out, layer_scale, cotangent,
):
    n_face, n_tile = lax.axis_size("face"), lax.axis_size("tile")
    n1, n2 = n_face * SUB, n_tile // SUB
    S, C = state_field.shape[0], state_field.shape[2]
    ks = depth_kernel.shape[0]
    m = ks // 2
    hid = weight_in.shape[1]
    taps = -(-ks * ks // 16) * 16
    rows = -(-(2 * hid + taps) // (16 * n1)) * 16
    rim = -(-(S + 2 * m) // 8) * 8
    scale = 1.0 / math.sqrt(S * S * n_face * n_tile)
    vmem = pl.BlockSpec(memory_space=pltpu.VMEM)
    dma = pltpu.SemaphoreType.DMA
    V = pltpu.VMEM
    line = lambda v: v.reshape(1, -1)
    block_out, grad_field, g_in, g_out, g_kern = pl.pallas_call(
        functools.partial(block_kernel, n_face, n_tile, rows, scale, S, ks),
        out_shape=(
            jax.ShapeDtypeStruct(state_field.shape, BF16),
            jax.ShapeDtypeStruct(state_field.shape, BF16),
            jax.ShapeDtypeStruct(weight_in.shape, F32),
            jax.ShapeDtypeStruct(weight_out.shape, F32),
            jax.ShapeDtypeStruct(depth_kernel.shape, F32),
        ),
        in_specs=[pl.BlockSpec(memory_space=pltpu.SMEM)] + [vmem] * 11,
        out_specs=[vmem] * 5,
        scratch_shapes=[
            V((S + 2 * m, S + 16, C), F32),
            V((ks, S + 2 * m, S, C), F32),
            V((ks, S + 4 * m, rim, C), F32),
            V((S + 2 * m, rim, C), F32),
            V((2 * m, rim, C), F32),
            V((taps, 8, C), F32),
            V((C, hid), F32),
            V((C, hid), F32),
            V((2, m, S, C), BF16), V((2, m, S, C), BF16),
            V((2, m, S + 16, C), BF16), V((2, m, S + 16, C), BF16),
            V((2, m, 64, C), BF16), V((2, m, 64, C), BF16),
            V((2, m, S, C), BF16), V((2, m, S, C), BF16),
            V((n1 * rows, C), BF16),
            V((n1 - 1, rows, C), BF16),
            V((n2, rows, C), BF16),
            V((n1 * rows, C), BF16),
            dma((8,)), dma((8,)),
            dma((n1 - 1,)), dma((n1 - 1,)), dma((n2 - 1,)), dma((n2 - 1,)), dma((n1 - 1,)), dma((n1 - 1,)),
        ],
        compiler_params=pltpu.CompilerParams(collective_id=0, has_side_effects=True, vmem_limit_bytes=56 << 20),
    )(
        turn_codes.reshape(-1), state_field, cotangent, depth_kernel,
        line(conv_bias), line(norm_gain), line(norm_shift), weight_in, line(bias_in),
        weight_out, line(bias_out), line(layer_scale),
    )
    return (block_out, grad_field, g_in, g_out, g_kern)


def solution(mesh):
    placed = (
        P("face", "tile", None),
        P("face", "tile", None),
        P(),
        P(),
        P(),
        P(),
        P(),
        P(),
        P(),
        P(),
        P(),
        P("face", "tile", None),
    )
    return jax.shard_map(
        body,
        mesh=mesh,
        in_specs=placed,
        out_specs=(P("face", "tile", None), P("face", "tile", None), P(), P(), P()),
        check_vma=False,
    )
```

```python
import functools
import math

import jax
import jax.numpy as jnp
from jax import lax
from jax.experimental import pallas as pl
from jax.experimental.pallas import tpu as pltpu
from jax.sharding import PartitionSpec as P

MESH_ID = pl.DeviceIdType.MESH
SUB = 4
F32 = jnp.float32
BF16 = jnp.bfloat16


def block_kernel(
    n_face, n_tile, rows, scale, side, ks,
    codes, x_ref, cot_ref, dk_ref, cb_ref, gain_ref, shift_ref, win_ref, bin_ref, wout_ref, bout_ref, ls_ref,
    out_ref, gf_ref, o_in, o_out, o_kern,
    xpad, xs, gs, pg, hold, kacc, acc_in, acc_out,
    col_send, col_recv, row_send, row_recv, grow_send, grow_recv, gcol_send, gcol_recv,
    send_buf, first_buf, second_buf, all_buf,
    halo_s, halo_r, send1, recv1, send2, recv2, send3, recv3,
):
    m = ks // 2
    S = side
    wide = S + 2 * m
    C = x_ref.shape[2]
    face, tile = lax.axis_index("face"), lax.axis_index("tile")
    n1, n2 = n_face * SUB, n_tile // SUB
    me1 = face * SUB + tile % SUB
    me2 = tile // SUB
    east, west = (face, (tile + 1) % n_tile), (face, (tile + n_tile - 1) % n_tile)
    below, above = ((face + 1) % n_face, tile), ((face + n_face - 1) % n_face, tile)

    def peer1(offset):
        other = (me1 + offset) % n1
        return other, (other // SUB, me2 * SUB + other % SUB)

    def peer2(offset):
        return (face, ((me2 + offset) % n2) * SUB + tile % SUB)

    barrier = pltpu.get_barrier_semaphore()
    for where in (east, west, below, above):
        pl.semaphore_signal(barrier, inc=1, device_id=where, device_id_type=MESH_ID)
    for k in range(1, n1):
        pl.semaphore_signal(barrier, inc=1, device_id=peer1(k)[1], device_id_type=MESH_ID)
    for k in range(1, n2):
        pl.semaphore_signal(barrier, inc=1, device_id=peer2(k), device_id_type=MESH_ID)

    def remote(src, dst, sems, index, where):
        copy = pltpu.make_async_remote_copy(
            src_ref=src, dst_ref=dst, send_sem=sems[0].at[index], recv_sem=sems[1].at[index],
            device_id=where, device_id_type=MESH_ID)
        copy.start()
        return copy

    halo = (halo_s, halo_r)
    q = [codes[i] for i in range(4)]

    def mirror(n, k, total):
        r = lax.broadcasted_iota(jnp.int32, (n, k), 0)
        c = lax.broadcasted_iota(jnp.int32, (n, k), 1)
        return jnp.where(r + c == total, 1.0, 0.0).astype(BF16)

    def flip(perm, value):
        return jnp.dot(perm, value.astype(BF16), preferred_element_type=F32)

    edge = jnp.zeros((wide, 8, C), F32)
    xpad[:, 0:8] = edge
    xpad[:, S + 8 : S + 16] = edge

    @pl.loop(0, S // 8)
    def _(i):
        xpad[pl.ds(m + i * 8, 8), 8 : 8 + S] = x_ref[pl.ds(i * 8, 8)].astype(F32)

    perm_s = mirror(S, S, S - 1)

    def col(j):
        return xpad[m : m + S, 8 + j, :]

    def row(j):
        return xpad[m + j, 8 : 8 + S, :]

    def turned(code, options):
        src = jnp.where(code == 1, options[1], options[0])
        src = jnp.where(code == 2, options[2], src)
        src = jnp.where(code == 3, options[3], src)
        return jnp.where((code == 1) | (code == 2), flip(perm_s, src), src)

    cols = {j: col(j) for j in list(range(m)) + list(range(S - m, S))}
    lines = {j: row(j) for j in list(range(m)) + list(range(S - m, S))}
    for j in range(m):
        hi, lo, opp = S - m + j, m - 1 - j, S - 1 - j
        col_send[0, j] = turned(q[0], [cols[hi], lines[hi], cols[lo], lines[lo]]).astype(BF16)
        col_send[1, j] = turned(q[1], [cols[j], lines[j], cols[opp], lines[opp]]).astype(BF16)
    pl.semaphore_wait(barrier, n1 + n2 + 2)
    halo_copies = [
        remote(col_send.at[0], col_recv.at[0], halo, 0, east),
        remote(col_send.at[1], col_recv.at[1], halo, 1, west),
    ]

    rim = gs.shape[2]

    @pl.loop(0, ks)
    def _(b):
        gs[b, 0 : 2 * m] = jnp.zeros((2 * m, rim, C), F32)
        gs[b, S + 2 * m :] = jnp.zeros((2 * m, rim, C), F32)

        @pl.loop(0, S // 8)
        def _(i):
            gs[b, pl.ds(2 * m + i * 8, 8), 0:8] = jnp.zeros((8, 8, C), F32)
            gs[b, pl.ds(2 * m + i * 8, 8), S : S + 8] = jnp.zeros((8, 8, C), F32)

    kacc[...] = jnp.zeros(kacc.shape, F32)
    acc_in[...] = jnp.zeros(acc_in.shape, F32)
    acc_out[...] = jnp.zeros(acc_out.shape, F32)

    def shifted(first, count):
        for b in range(ks):
            xs[b, pl.ds(first, count)] = xpad[pl.ds(first, count), 8 - m + b : 8 - m + b + S]

    halo_copies[0].wait_recv()
    halo_copies[1].wait_recv()
    for j in range(m):
        xpad[m : m + S, 8 - m + j, :] = col_recv[0, j].astype(F32)
        xpad[m : m + S, 8 + S + j, :] = col_recv[1, j].astype(F32)
    perm_w = mirror(S + 16, S + 16, S + 15)
    for i in range(m):
        south = jnp.where(q[2] % 2 == 0, xpad[S + i], flip(perm_w, xpad[2 * m - 1 - i]))
        north = jnp.where(q[3] % 2 == 0, xpad[m + i], flip(perm_w, xpad[m + S - 1 - i]))
        row_send[0, i] = south.astype(BF16)
        row_send[1, i] = north.astype(BF16)
    halo_copies += [
        remote(row_send.at[0], row_recv.at[0], halo, 2, below),
        remote(row_send.at[1], row_recv.at[1], halo, 3, above),
    ]

    @pl.loop(0, S // 6)
    def _(i):
        shifted(m + i * 6, 6)

    R = 8
    M = R * S
    contract0 = (((0,), (0,)), ((), ()))
    contract1 = (((1,), (1,)), ((), ()))

    def pointwise(i):
        i0 = i * R
        parts = []
        for s in range(0, R, 4):
            acc = jnp.zeros((4, S, C), F32)
            for a in range(ks):
                for b in range(ks):
                    acc = acc + xs[b, pl.ds(i0 + s + a, 4)] * dk_ref[a, b : b + 1]
            parts.append(acc.reshape(4 * S, C))
        conv = jnp.concatenate(parts, axis=0) + cb_ref[...]
        center = conv - jnp.mean(conv, axis=-1, keepdims=True)
        inverse = lax.rsqrt(jnp.mean(center * center, axis=-1, keepdims=True) + 1e-06)
        normed = center * inverse
        gain = gain_ref[...]
        norm_rows = (normed * gain + shift_ref[...]).astype(BF16)
        hidden = jnp.dot(norm_rows, win_ref[...], preferred_element_type=F32) + bin_ref[...]
        cdf = 0.5 * (1.0 + lax.erf(hidden * 0.7071067811865476))
        pdf = jnp.exp(-0.5 * hidden * hidden) * 0.3989422804014327
        active = (hidden * cdf).astype(BF16)
        mixed = jnp.dot(active, wout_ref[...], preferred_element_type=F32) + bout_ref[...]
        tile_in = x_ref[pl.ds(i0, R)].astype(F32).reshape(M, C)
        out_ref[pl.ds(i0, R)] = (tile_in + ls_ref[...] * mixed).astype(BF16).reshape(R, S, C)
        cot = cot_ref[pl.ds(i0, R)].astype(F32).reshape(M, C)
        grad_mixed = (cot * ls_ref[...]).astype(BF16)
        acc_out[...] += lax.dot_general(grad_mixed, active, contract0, preferred_element_type=F32)
        grad_active = lax.dot_general(grad_mixed, wout_ref[...], contract1, preferred_element_type=F32)
        grad_hidden = (grad_active * (cdf + hidden * pdf)).astype(BF16)
        acc_in[...] += lax.dot_general(norm_rows, grad_hidden, contract0, preferred_element_type=F32)
        gn = lax.dot_general(grad_hidden, win_ref[...], contract1, preferred_element_type=F32) * gain
        g = inverse * (
            gn - jnp.mean(gn, axis=-1, keepdims=True)
            - normed * jnp.mean(gn * normed, axis=-1, keepdims=True)
        )
        g = g.reshape(R, S, C)
        for b in range(ks):
            gs[b, pl.ds(i0 + 2 * m, R), b : b + S] = g

    @pl.loop(1, S // R - 1)
    def _(i):
        pointwise(i)

    halo_copies[2].wait_recv()
    halo_copies[3].wait_recv()
    xpad[0:m] = row_recv[0].astype(F32)
    xpad[m + S :] = row_recv[1].astype(F32)
    shifted(0, m)
    shifted(m + S, m)

    @pl.loop(0, 2)
    def _(e):
        pointwise(e * (S // R - 1))

    def spread(p, count, first, width):
        acc = jnp.zeros((count, width, C), F32)
        for a in range(ks):
            for b in range(ks):
                acc = acc + gs[b, pl.ds(p + 2 * m - a, count), first : first + width] * dk_ref[a, b : b + 1]
        pg[pl.ds(p, count), first : first + width] = acc

    @pl.loop(0, 2)
    def _(e):
        spread(e * (S + m), m, 0, rim)

    gap = jnp.zeros((m, 64 - rim, C), F32)
    grow_send[0] = jnp.concatenate([pg[0:m], gap], axis=1).astype(BF16)
    grow_send[1] = jnp.concatenate([pg[S + m :], gap], axis=1).astype(BF16)
    halo_copies += [
        remote(grow_send.at[0], grow_recv.at[0], halo, 4, above),
        remote(grow_send.at[1], grow_recv.at[1], halo, 5, below),
    ]

    @pl.loop(0, S // 4)
    def _(i):
        g = gs[0, pl.ds(i * 4 + 2 * m, 4), 0:S]
        for a in range(ks):
            for b in range(ks):
                prod = xs[b, pl.ds(i * 4 + a, 4)] * g
                kacc[a * ks + b] += jnp.sum(prod.reshape(S // 2, 8, C), axis=0)

    blocks = acc_in.shape[1] // 128
    base = blocks * 128
    for k in range(blocks):
        send_buf[k * 128 : (k + 1) * 128] = acc_in[:, k * 128 : (k + 1) * 128].astype(BF16)
        send_buf[base + k * 128 : base + (k + 1) * 128] = acc_out[:, k * 128 : (k + 1) * 128].T.astype(BF16)
    taps = kacc.shape[0]
    send_buf[2 * base : 2 * base + taps] = jnp.sum(kacc[...], axis=1).astype(BF16)
    if n1 * rows > 2 * base + taps:
        send_buf[2 * base + taps :] = jnp.zeros((n1 * rows - 2 * base - taps, 128), BF16)

    def part(index):
        return pl.ds(pl.multiple_of(index * rows, 16), rows)

    copies = []
    for k in range(1, n1):
        other, where = peer1(k)
        copies.append(remote(send_buf.at[part(other)], first_buf.at[k - 1], (send1, recv1), k - 1, where))

    @pl.loop(0, S // 12)
    def _(i):
        spread(m + i * 12, 12, 0, 8)
        spread(m + i * 12, 12, rim - 8, 8)

    halo_copies[4].wait_recv()
    halo_copies[5].wait_recv()
    perm_r = mirror(rim, 64, wide - 1)
    for i in range(m):
        top_turned = flip(perm_r, grow_recv[0, m - 1 - i])
        end_turned = flip(perm_r, grow_recv[1, m - 1 - i])
        north = grow_recv[1, i].astype(F32)[:rim]
        south = grow_recv[0, i].astype(F32)[:rim]
        hold[i] = jnp.where(q[3] % 2 == 0, north, 0.0) + jnp.where(q[2] % 2 == 1, top_turned, 0.0)
        hold[m + i] = jnp.where(q[3] % 2 == 1, end_turned, 0.0) + jnp.where(q[2] % 2 == 0, south, 0.0)

    def add_rows(first, width):
        for start, at in ((m, 0), (S, m)):
            pg[start : start + m, first : first + width] += hold[at : at + m, first : first + width]

    add_rows(0, 8)
    add_rows(rim - 8, 8)
    for j in range(m):
        gcol_send[0, j] = pg[m : m + S, j, :].astype(BF16)
        gcol_send[1, j] = pg[m : m + S, S + m + j, :].astype(BF16)
    halo_copies += [
        remote(gcol_send.at[0], gcol_recv.at[0], halo, 6, west),
        remote(gcol_send.at[1], gcol_recv.at[1], halo, 7, east),
    ]

    total = send_buf[part(me1)].astype(F32)
    for k in range(1, n1):
        copies[k - 1].wait_recv()
        total = total + first_buf[k - 1].astype(F32)
    second_buf[me2] = total.astype(BF16)
    copies2 = []
    for k in range(1, n2):
        copies2.append(remote(second_buf.at[me2], second_buf.at[me2], (send2, recv2), k - 1, peer2(k)))

    middle = S // 8

    @pl.loop(0, middle)
    def _(i):
        spread(m + i * 4, 4, 8, rim - 16)

    for copy in copies2:
        copy.wait_recv()
    total = second_buf[0].astype(F32)
    for k in range(1, n2):
        total = total + second_buf[k].astype(F32)
    all_buf[part(me1)] = total.astype(BF16)
    copies3 = []
    for k in range(1, n1):
        copies3.append(
            remote(all_buf.at[part(me1)], all_buf.at[part(me1)], (send3, recv3), k - 1, peer1(k)[1])
        )

    @pl.loop(middle, S // 4)
    def _(i):
        spread(m + i * 4, 4, 8, rim - 16)

    add_rows(8, rim - 16)
    halo_copies[6].wait_recv()
    halo_copies[7].wait_recv()

    def back(code, value):
        plain = value.astype(F32)
        return jnp.where((code == 1) | (code == 2), flip(perm_s, value), plain)

    from_east = [back(q[0], gcol_recv[0, j]) for j in range(m)]
    from_west = [back(q[1], gcol_recv[1, j]) for j in range(m)]

    def pair(east_code, east_value, west_code, west_value):
        return jnp.where(q[0] == east_code, east_value, 0.0) + jnp.where(q[1] == west_code, west_value, 0.0)

    for j in range(m):
        o = m - 1 - j
        hi = S - m + j
        pg[m : m + S, m + hi, :] += pair(0, from_east[j], 2, from_west[o])
        pg[m : m + S, m + j, :] += pair(2, from_east[o], 0, from_west[j])
        pg[m + hi, m : m + S, :] += pair(1, from_east[j], 3, from_west[o])
        pg[m + j, m : m + S, :] += pair(3, from_east[o], 1, from_west[j])

    @pl.loop(0, S // 8)
    def _(i):
        cells = pg[pl.ds(m + i * 8, 8), m : m + S]
        gf_ref[pl.ds(i * 8, 8)] = (cot_ref[pl.ds(i * 8, 8)].astype(F32) + cells).astype(BF16)

    for copy in copies3:
        copy.wait_recv()
    for copy in halo_copies + copies + copies2 + copies3:
        copy.wait_send()
    for k in range(blocks):
        o_in[:, k * 128 : (k + 1) * 128] = all_buf[k * 128 : (k + 1) * 128]
    o_out[...] = all_buf[base : 2 * base]
    kern = all_buf[2 * base : 2 * base + taps].astype(F32) * scale
    for a in range(ks):
        o_kern[a] = kern[a * ks : (a + 1) * ks]


def body(
    state_field, turn_codes, depth_kernel, conv_bias, norm_gain, norm_shift,
    weight_in, bias_in, weight_out, bias_out, layer_scale, cotangent,
):
    n_face, n_tile = lax.axis_size("face"), lax.axis_size("tile")
    n1, n2 = n_face * SUB, n_tile // SUB
    S, C = state_field.shape[0], state_field.shape[2]
    ks = depth_kernel.shape[0]
    m = ks // 2
    hid = weight_in.shape[1]
    taps = -(-ks * ks // 16) * 16
    rows = -(-(2 * hid + taps) // (16 * n1)) * 16
    rim = -(-(S + 2 * m) // 8) * 8
    scale = 1.0 / math.sqrt(S * S * n_face * n_tile)
    vmem = pl.BlockSpec(memory_space=pltpu.VMEM)
    dma = pltpu.SemaphoreType.DMA
    V = pltpu.VMEM
    line = lambda v: v.reshape(1, -1)
    block_out, grad_field, g_in, g_out, g_kern = pl.pallas_call(
        functools.partial(block_kernel, n_face, n_tile, rows, scale, S, ks),
        out_shape=(
            jax.ShapeDtypeStruct(state_field.shape, BF16),
            jax.ShapeDtypeStruct(state_field.shape, BF16),
            jax.ShapeDtypeStruct(weight_in.shape, BF16),
            jax.ShapeDtypeStruct(weight_out.shape, BF16),
            jax.ShapeDtypeStruct(depth_kernel.shape, F32),
        ),
        in_specs=[pl.BlockSpec(memory_space=pltpu.SMEM)] + [vmem] * 11,
        out_specs=[vmem] * 5,
        scratch_shapes=[
            V((S + 2 * m, S + 16, C), F32),
            V((ks, S + 2 * m, S, C), F32),
            V((ks, S + 4 * m, rim, C), F32),
            V((S + 2 * m, rim, C), F32),
            V((2 * m, rim, C), F32),
            V((taps, 8, C), F32),
            V((C, hid), F32),
            V((C, hid), F32),
            V((2, m, S, C), BF16), V((2, m, S, C), BF16),
            V((2, m, S + 16, C), BF16), V((2, m, S + 16, C), BF16),
            V((2, m, 64, C), BF16), V((2, m, 64, C), BF16),
            V((2, m, S, C), BF16), V((2, m, S, C), BF16),
            V((n1 * rows, C), BF16),
            V((n1 - 1, rows, C), BF16),
            V((n2, rows, C), BF16),
            V((n1 * rows, C), BF16),
            dma((8,)), dma((8,)),
            dma((n1 - 1,)), dma((n1 - 1,)), dma((n2 - 1,)), dma((n2 - 1,)), dma((n1 - 1,)), dma((n1 - 1,)),
        ],
        compiler_params=pltpu.CompilerParams(collective_id=0, has_side_effects=True, vmem_limit_bytes=56 << 20),
    )(
        turn_codes.reshape(-1), state_field, cotangent, depth_kernel,
        line(conv_bias), line(norm_gain), line(norm_shift), weight_in, line(bias_in),
        weight_out, line(bias_out), line(layer_scale),
    )
    return (block_out, grad_field, g_in.astype(F32) * scale, g_out.astype(F32) * scale, g_kern)


def solution(mesh):
    placed = (
        P("face", "tile", None),
        P("face", "tile", None),
        P(),
        P(),
        P(),
        P(),
        P(),
        P(),
        P(),
        P(),
        P(),
        P("face", "tile", None),
    )
    return jax.shard_map(
        body,
        mesh=mesh,
        in_specs=placed,
        out_specs=(P("face", "tile", None), P("face", "tile", None), P(), P(), P()),
        check_vma=False,
    )
```
